32 devices in a mesh: seq: 16 (over z, y, core), ch: 2 (over x).
Axes of the slice: x: 2, y: 2, z: 4, core: 2. Of those that a mesh axis runs over, the one named last changes fastest.
Arguments:
- gate_in: bfloat16 [4096, 4096], P('seq', 'ch'), may hold values from -80 to 80
- key_in: bfloat16 [4096, 4096], P('seq', 'ch'), may hold values from -6 to 6
- value_in: bfloat16 [4096, 4096], P('seq', 'ch'), may hold values from -6 to 6
- long_filter: bfloat16 [4096, 4096], P('seq', 'ch'), may hold values from -2 to 2
- gate_short: float32 [3, 4096], P(None, 'ch'), may hold values from -3 to 3
- key_short: float32 [3, 4096], P(None, 'ch'), may hold values from -3 to 3
- value_short: float32 [3, 4096], P(None, 'ch'), may hold values from -3 to 3
- skip_gain: float32 [4096], P('ch'), may hold values from 0.5 to 1.5
- norm_gain: float32 [4096], P('ch'), may hold values from 0.5 to 1.5
Outputs:
- mixed: bfloat16 [4096, 4096], P('seq', 'ch')
The draws below stay inside these ranges and needn't reach their ends.
All inputs are finite; a program needn't handle non-finite values.
Results may differ from the reference program's by a relative error of at most 0.0057.
Values may be sent and summed in bfloat16 or wider, within the bound.
No kernel may reach another device: no remote copies, remote signals or barrier semaphores. Data moves between devices by JAX's collectives and lax.ppermute only.
A program may use at most 128 MiB of HBM per device.

```python
import math
import jax
import jax.numpy as jnp
from jax import lax

D = 4096
TAPS = 3
SEQLEN = 4096


def draw_gate_in(key, part):
    first, second, third = jax.random.split(key, 3)
    rowscale = jnp.exp(jax.random.uniform(second, (SEQLEN, 1), minval=0.0, maxval=math.log(10.0)))
    spread = jax.random.uniform(third, (1, D))
    ramp = jnp.arange(D, dtype=jnp.float32)[None, :] / D
    base = jax.random.normal(first, (SEQLEN, D))
    colscale = 10.0 ** (0.6 * ramp + 0.4 * spread)
    return jnp.clip(base * rowscale * colscale / 10.0, -70.0, 70.0).astype(jnp.bfloat16)


def draw_long_filter(key, part):
    key = jax.random.fold_in(key, 7)
    first, second, third, fourth, fifth = jax.random.split(key, 5)
    lags = jnp.arange(SEQLEN, dtype=jnp.float32)[:, None]
    choose = jax.random.uniform(second, (1, D))
    slow_tau = jnp.exp(jax.random.uniform(third, (1, D), minval=math.log(SEQLEN / 2.0), maxval=math.log(20.0 * SEQLEN)))
    fast_tau = jnp.exp(jax.random.uniform(fourth, (1, D), minval=math.log(20.0), maxval=math.log(200.0)))
    decay = jnp.where(choose < 0.5, slow_tau, fast_tau)
    amplitude = 0.8 / jnp.sqrt(jnp.minimum(decay, float(SEQLEN)))
    tail_amp = 0.2 / math.sqrt(float(SEQLEN))
    noise = jnp.clip(jax.random.normal(first, (SEQLEN, D)), -6.0, 6.0)
    tail = jnp.clip(jax.random.normal(fifth, (SEQLEN, D)), -6.0, 6.0)
    taps = noise * amplitude * jnp.exp(-lags / decay) + tail_amp * tail
    return jnp.clip(taps, -1.9, 1.9).astype(jnp.bfloat16)


def shard_levels(stream_key, dims, cuts, smallest, largest):
    loudness, own = 1.0, jax.random.fold_in(stream_key, 6)
    for axis_at, blocks in cuts:
        steps = jnp.exp(jax.random.uniform(jax.random.fold_in(own, axis_at), (blocks,), jnp.float32, smallest / len(cuts), largest / len(cuts)))
        loudness = loudness * jnp.repeat(steps, dims[axis_at] // blocks).reshape([-1 if axis == axis_at else 1 for axis in range(len(dims))])
    return loudness


def centred(own_key, dims, scale, limit, cuts=(), kind=jnp.bfloat16):
    values = scale * jax.random.normal(own_key, dims, jnp.float32)
    if cuts:
        values = values * shard_levels(own_key, dims, cuts, -0.22, 0.18)
    return jnp.clip(values, -limit, limit).astype(kind)


def setup_inputs(seed: int = 0) -> dict:
    seeds = jax.random.split(jax.random.key(seed), 10)
    gate_in = draw_gate_in(jax.random.fold_in(seeds[9], 71), 0)
    key_in = centred(seeds[1], (SEQLEN, D), 1.0, 6.0, ((0, 16), (1, 2)))
    value_in = centred(seeds[2], (SEQLEN, D), 1.0, 6.0, ((0, 16), (1, 2)))
    long_filter = draw_long_filter(jax.random.fold_in(seeds[9], 71), 0)
    gate_short = centred(seeds[4], (TAPS, D), 0.7, 3.0, ((1, 2),), jnp.float32)
    key_short = centred(seeds[5], (TAPS, D), 0.7, 3.0, ((1, 2),), jnp.float32)
    value_short = centred(seeds[6], (TAPS, D), 0.7, 3.0, ((1, 2),), jnp.float32)
    skip_gain = jnp.clip(0.5 + 1.0 * jax.random.uniform(seeds[7], (D,), jnp.float32) ** shard_levels(seeds[7], (D,), ((0, 2),), -0.2, 0.2), 0.5, 1.5)
    norm_gain = jnp.clip(1.0 + 0.1 * jax.random.normal(seeds[8], (D,), jnp.float32), 0.5, 1.5)
    return {"gate_in": gate_in, "key_in": key_in, "value_in": value_in, "long_filter": long_filter, "gate_short": gate_short, "key_short": key_short, "value_short": value_short, "skip_gain": skip_gain, "norm_gain": norm_gain}


def short_conv(rows, taps):
    padded = jnp.pad(rows, ((2, 0), (0, 0)))
    return taps[0] * rows + taps[1] * padded[1:-1] + taps[2] * padded[:-2]

def lane_conv(pair):
    left, right = pair
    left_spec = jnp.fft.rfft(left, n=2 * SEQLEN, axis=0)
    right_spec = jnp.fft.rfft(right, n=2 * SEQLEN, axis=0)
    return jnp.fft.irfft(left_spec * right_spec, n=2 * SEQLEN, axis=0)[:SEQLEN]

def reference(gate_in, key_in, value_in, long_filter, gate_short, key_short, value_short, skip_gain, norm_gain):
    gate_conv = short_conv(gate_in.astype(jnp.float32), gate_short.astype(jnp.float32))
    key_conv = short_conv(key_in.astype(jnp.float32), key_short.astype(jnp.float32))
    value_conv = short_conv(value_in.astype(jnp.float32), value_short.astype(jnp.float32))
    product = (key_conv * value_conv).astype(jnp.bfloat16)
    width = math.gcd(D, 256)
    blocks = D // width
    left = product.astype(jnp.float32).reshape(SEQLEN, blocks, width).transpose(1, 0, 2)
    right = long_filter.astype(jnp.float32).reshape(SEQLEN, blocks, width).transpose(1, 0, 2)
    conv = lax.map(lane_conv, (left, right)).transpose(1, 0, 2).reshape(SEQLEN, D)
    mixed_in = (conv + skip_gain.astype(jnp.float32)[None, :] * product.astype(jnp.float32)).astype(jnp.bfloat16)
    gated = gate_conv * mixed_in.astype(jnp.float32)
    meansq = lax.optimization_barrier(jnp.mean(gated * gated, axis=1, keepdims=True))
    return (gated * norm_gain.astype(jnp.float32)[None, :] * lax.rsqrt(meansq + 1e-06)).astype(jnp.bfloat16)
```

```python
import functools

import jax
import jax.numpy as jnp
from jax import lax
from jax.experimental import pallas as pl
from jax.experimental.pallas import tpu as pltpu
from jax.sharding import PartitionSpec as P

LANES = 128
FINE = 32
GROUP = 4
HALO = 16
WIDE = 512
PARTS = 2
NEAR = 4
VMEM_BYTES = 20 * 1024 * 1024
F32 = jnp.float32
BF16 = jnp.bfloat16


def passed_along(array, axis, by):
    size = lax.axis_size(axis)
    pairs = [(i, i + by) for i in range(size) if 0 <= i + by < size]
    return lax.ppermute(array, axis, pairs)


def short_conv(rows, prev, taps):
    last = prev[HALO - 1 : HALO]
    before = prev[HALO - 2 : HALO - 1]
    at = lax.broadcasted_iota(jnp.int32, rows.shape, 0)
    one = jnp.where(at == 0, last, pltpu.roll(rows, 1, 0))
    two = jnp.where(at == 0, before, jnp.where(at == 1, last, pltpu.roll(rows, 2, 0)))
    return taps[0:1] * rows + taps[1:2] * one + taps[2:3] * two


def send_out(held, outs, origin):
    for near, out_ref in enumerate(outs):
        for far in range(out_ref.shape[0]):
            out_ref[far] = held[origin ^ (far * len(outs) + near)]


def pack_kernel(wants, at_ref, *refs):
    refs, outs, held = refs[: -NEAR - 1], refs[-NEAR - 1 : -1], refs[-1]
    blocks, _, narrow, tok = held.shape
    count = WIDE // narrow
    step = pl.program_id(0)
    here = pl.ds(step * count, count)
    refs = list(refs)
    for at, want in enumerate(wants):
        if want == "filter":
            packed = refs.pop(0)[...].astype(F32)
        else:
            key, value, halo, key_taps, value_taps = [refs.pop(0)[...] for _ in range(5)]
            halo = halo.astype(F32)
            packed = short_conv(key.astype(F32), halo[:HALO], key_taps)
            packed *= short_conv(value.astype(F32), halo[HALO : 2 * HALO], value_taps)
        held[here, at] = packed.T.astype(BF16).reshape(count, narrow, tok)

    @pl.when(step == pl.num_programs(0) - 1)
    def _():
        for near, out_ref in enumerate(outs):
            for far in range(blocks // NEAR):
                out_ref[far] = held[at_ref[0] ^ (far * NEAR + near)]


def packed(wants, arrays, part, position):
    start, narrow, blocks = part
    tok = arrays[0].shape[0]
    first = start // WIDE
    shape = (blocks // NEAR, len(wants), narrow, tok)
    return pl.pallas_call(
        functools.partial(pack_kernel, wants),
        grid_spec=pltpu.PrefetchScalarGridSpec(
            num_scalar_prefetch=1,
            grid=(blocks * narrow // WIDE,),
            in_specs=[
                pl.BlockSpec((array.shape[0], WIDE), lambda i, at: (0, first + i))
                for array in arrays
            ],
            out_specs=[pl.BlockSpec(shape, lambda i, at: (0, 0, 0, 0))] * NEAR,
            scratch_shapes=[pltpu.VMEM((blocks,) + shape[1:], BF16)],
        ),
        out_shape=[jax.ShapeDtypeStruct(shape, BF16)] * NEAR,
        compiler_params=pltpu.CompilerParams(vmem_limit_bytes=VMEM_BYTES),
        cost_estimate=pl.CostEstimate(
            flops=8 * len(arrays) * tok * blocks * narrow,
            bytes_accessed=4 * len(arrays) * tok * blocks * narrow,
            transcendentals=0,
        ),
        name="pack_" + "_".join(wants),
    )(position, *arrays)


def swapped(rows, by):
    size = lax.axis_size("seq")
    return lax.ppermute(rows, "seq", [(i, i ^ by) for i in range(size)])


def swap_near(parts):
    parts = [parts[0]] + [swapped(parts[i], i) for i in range(1, len(parts))]
    return [jnp.stack([part[j] for part in parts]) for j in range(parts[0].shape[0])]


def swap_far(lines):
    return [lines[0]] + [swapped(lines[j], NEAR * j) for j in range(1, len(lines))]


def swap_back(lines):
    lines = swap_far(lines)
    parts = [jnp.stack([line[i] for line in lines]) for i in range(NEAR)]
    return [parts[0]] + [swapped(parts[i], i) for i in range(1, NEAR)]


def delayed(rows, by):
    at = lax.broadcasted_iota(jnp.int32, rows.shape, 1)
    return jnp.where(at < by, 0.0, pltpu.roll(rows, by, 1))


def halves(first, second, upper):
    return (
        jnp.where(upper, first, pltpu.roll(second, 4, second.ndim - 2)),
        jnp.where(upper, pltpu.roll(first, 4, first.ndim - 2), second),
    )


def left_rows(pairs, turns):
    tok = pairs.shape[1]
    lane_of = lax.broadcasted_iota(jnp.int32, (turns * 8, LANES), 1) // FINE
    own = lane_of == lax.broadcasted_iota(jnp.int32, (turns * 8, LANES), 0) % GROUP
    columns = []
    for a in range(tok // LANES):
        piece = pairs[:, a * LANES : (a + 1) * LANES]
        moved = [piece] + [pltpu.roll(piece, FINE * d, 1) for d in range(1, 4)]
        picked = []
        for e in range(LANES // FINE):
            spread = moved[(3 - e) % 4]
            for c in range(3):
                spread = jnp.where(lane_of == c, moved[(c - e) % 4], spread)
            picked.append(jnp.where(own, spread, 0.0).reshape(turns, 1, 8, LANES))
        columns.append(jnp.concatenate(picked, axis=1).reshape(turns * 32, LANES).astype(BF16))
    return jnp.concatenate(columns, axis=1)


def conv_kernel(at_ref, skip_ref, *refs):
    refs, (filt, prod, base, left, total, held) = refs[:-6], refs[-6:]
    blocks, lanes, tok = prod.shape
    far = blocks // NEAR
    in_refs, out_refs = refs[:-far], refs[-far:]
    length = blocks * tok
    turns = blocks // 2
    units = lanes // 16

    merged = in_refs[0].shape[1] == 2
    for j in range(far):
        for i in range(NEAR):
            block = at_ref[0] ^ (NEAR * j + i)
            lags = pl.ds(pl.multiple_of(block * tok, tok), tok)
            filt[:, lags] = in_refs[j][i, 0].astype(F32)
            prod[block] = (in_refs[j][i, 1] if merged else in_refs[far + j][i, 0]).astype(F32)
    base[:, :, :LANES] = jnp.zeros((2, GROUP * FINE, LANES), BF16)

    def pairs_of(row, side):
        rows = prod[:, pl.ds(pl.multiple_of(row, 8), 8), :].reshape(turns, 2, 8, tok)
        upper = lax.broadcasted_iota(jnp.int32, (turns, 8, tok), 1) < 4
        return halves(rows[:, 0], rows[:, 1], upper)[side].reshape(turns * 8, tok)

    def build_left(row, side):
        left[side] = left_rows(pairs_of(row, side), turns)

    def build_base(row, side, c, pair):
        line = jnp.broadcast_to(filt[pl.ds(row + side * GROUP + c, 1), :], (8, length))
        steps = []
        for a in (2 * pair, 2 * pair + 1):
            shifted = pltpu.roll(line, 8 * a, 1, stride=1, stride_axis=0)
            late = lax.broadcasted_iota(
                jnp.int32, (8, LANES), 1
            ) >= 8 * a + lax.broadcasted_iota(jnp.int32, (8, LANES), 0)
            steps.append(
                jnp.concatenate(
                    [jnp.where(late, shifted[:, :LANES], 0.0), shifted[:, LANES:]], axis=1
                )
            )
        at = c * FINE + 16 * pair
        base[side, at : at + 16, LANES:] = jnp.concatenate(steps, axis=0).astype(BF16)

    jobs = [(c, pair) for c in range(GROUP) for pair in range(FINE // 16)]

    def multiply(side, k):
        start = k * tok
        right = jnp.concatenate(
            [
                base[side, :, LANES + start : LANES + start + tok],
                base[side, :, start : start + tok],
            ],
            axis=0,
        )
        count = turns - k // 2
        out = jnp.dot(left[side, : 32 * count], right, preferred_element_type=F32)
        for m in range(count):
            at = slice(start + 2 * tok * m, start + 2 * tok * m + tok)
            piece = out[32 * m : 32 * m + 32]
            if k < 2:
                total[side, :, at] = piece
            else:
                total[side, :, at] += piece

    def summed(side):
        run = total[side, 24:32]
        for e in (2, 1, 0):
            run = total[side, 8 * e : 8 * e + 8] + delayed(run, FINE)
        return run

    build_left(0, 0)
    for job in jobs:
        build_base(0, 0, *job)

    def unit(index, carry):
        done = []
        for part in range(2):
            row = index * 16 + 8 * part
            sums = []
            for side in range(2):
                if side == 0:
                    after = row
                elif part == 0:
                    after = row + 8
                else:
                    after = jnp.minimum(row + 8, lanes - 8)
                build_left(after, 1 - side)
                for k in range(blocks):
                    for at, job in enumerate(jobs):
                        if at * blocks // len(jobs) == k:
                            build_base(after, 1 - side, *job)
                    multiply(side, k)
                sums.append(summed(side))
            upper = lax.broadcasted_iota(jnp.int32, (8, length), 0) < 4
            even, odd = halves(sums[0], sums[1], upper)
            conv = even + jnp.concatenate(
                [jnp.zeros((8, tok), F32), odd[:, : length - tok]], axis=1
            )
            here = pl.ds(pl.multiple_of(row, 8), 8)
            skip = jnp.concatenate([skip_ref[here, :]] * (tok // LANES), axis=1)
            done.append(
                [conv[:, h * tok : (h + 1) * tok] + skip * prod[h, here, :] for h in range(blocks)]
            )
        for h in range(blocks):
            held[h, pl.ds(pl.multiple_of(index * 16, 16), 16), :] = jnp.concatenate(
                [done[0][h], done[1][h]], axis=0
            ).astype(BF16)
        return carry

    lax.fori_loop(0, units, unit, 0)
    for j in range(far):
        for i in range(NEAR):
            out_refs[j][i] = held[at_ref[0] ^ (NEAR * j + i)]


def long_conv(arrays, skip_rows, blocks, position):
    near, _, lanes, tok = arrays[0].shape
    far = blocks // near
    length = blocks * tok
    whole = lambda array: pl.BlockSpec(array.shape, lambda i, at: (0,) * array.ndim)
    operands = [skip_rows, *arrays]
    out_shape = [jax.ShapeDtypeStruct((near, lanes, tok), BF16)] * far
    return pl.pallas_call(
        conv_kernel,
        grid_spec=pltpu.PrefetchScalarGridSpec(
            num_scalar_prefetch=1,
            grid=(1,),
            in_specs=[whole(array) for array in operands],
            out_specs=[whole(array) for array in out_shape],
            scratch_shapes=[
                pltpu.VMEM((lanes, length), F32),
                pltpu.VMEM((blocks, lanes, tok), F32),
                pltpu.VMEM((2, GROUP * FINE, LANES + length), BF16),
                pltpu.VMEM((2, 16 * blocks, 2 * LANES), BF16),
                pltpu.VMEM((2, 32, length), F32),
                pltpu.VMEM((blocks, lanes, tok), BF16),
            ],
        ),
        out_shape=out_shape,
        compiler_params=pltpu.CompilerParams(vmem_limit_bytes=VMEM_BYTES),
        cost_estimate=pl.CostEstimate(
            flops=64 * lanes * length * 256, bytes_accessed=6 * lanes * length, transcendentals=0
        ),
        name="long_conv",
    )(position, *operands)


def gated_kernel(at_ref, gate_ref, halo_ref, taps_ref, *refs):
    mixed_refs, refs, held = refs[:NEAR], refs[NEAR:-1], refs[-1]
    gated_ref, squares_ref = refs[-2:]
    _, narrow, tok = held.shape
    count = WIDE // narrow
    step = pl.program_id(0)

    @pl.when(step == 0)
    def _():
        for i, mixed_ref in enumerate(mixed_refs):
            for j in range(mixed_ref.shape[0]):
                held[at_ref[0] ^ (NEAR * j + i)] = mixed_ref[j]

    halo = halo_ref[...].astype(F32)
    gate = short_conv(gate_ref[...].astype(F32), halo[2 * HALO :], taps_ref[...])
    mixed = held[pl.ds(step * count, count)].reshape(WIDE, tok)
    gated = gate * mixed.astype(F32).T
    gated_ref[...] = gated
    squares = gated * gated
    part = squares[:, :LANES]
    for at in range(LANES, WIDE, LANES):
        part = part + squares[:, at : at + LANES]
    turned = jnp.sum(part.T.reshape(LANES // 8, 8, part.shape[0]), axis=0)

    @pl.when(step == 0)
    def _():
        squares_ref[...] = refs[0][...] + turned if len(refs) > 2 else turned

    @pl.when(step > 0)
    def _():
        squares_ref[...] += turned


def gated_of(gate_in, halo, gate_short, mixed, start, before, position):
    tok, full = gate_in.shape
    far, narrow, _ = mixed[0].shape
    width = NEAR * far * narrow
    first = start // WIDE
    column = lambda rows: pl.BlockSpec((rows, WIDE), lambda i, at: (0, first + i))
    sums = pl.BlockSpec((8, tok), lambda i, at: (0, 0))
    more = [] if before is None else [sums, pl.BlockSpec(memory_space=pl.ANY)]
    return pl.pallas_call(
        gated_kernel,
        grid_spec=pltpu.PrefetchScalarGridSpec(
            num_scalar_prefetch=1,
            grid=(width // WIDE,),
            in_specs=[column(tok), column(3 * HALO), column(3)]
            + [pl.BlockSpec(mixed[0].shape, lambda i, at: (0, 0, 0))] * NEAR
            + more,
            out_specs=[column(tok), sums],
            scratch_shapes=[pltpu.VMEM((NEAR * far, narrow, tok), BF16)],
        ),
        out_shape=[
            jax.ShapeDtypeStruct((tok, full), F32),
            jax.ShapeDtypeStruct((8, tok), F32),
        ],
        input_output_aliases={5 + NEAR: 0} if more else {},
        compiler_params=pltpu.CompilerParams(vmem_limit_bytes=VMEM_BYTES),
        cost_estimate=pl.CostEstimate(
            flops=10 * tok * width, bytes_accessed=8 * tok * width, transcendentals=0
        ),
        name="gated_squares",
    )(
        position,
        gate_in,
        halo,
        gate_short,
        *mixed,
        *(() if before is None else (before[1], before[0])),
    )


def norm_kernel(channels, gated_ref, gain_ref, *refs):
    sums, out_ref = refs[:-1], refs[-1]
    total = sums[0][...]
    for other in sums[1:]:
        total = total + other[...]
    total = jnp.sum(total, axis=0, keepdims=True)
    scale = lax.rsqrt(total / channels + 1e-06)
    scale = jnp.broadcast_to(scale, (LANES, scale.shape[1])).T
    scale = jnp.concatenate([scale] * (WIDE // LANES), axis=1)
    out_ref[...] = (gated_ref[...] * gain_ref[...] * scale).astype(BF16)


def normed(gated, squares, norm_gain, channels):
    tok, width = gated.shape
    column = lambda rows: pl.BlockSpec((rows, WIDE), lambda i: (0, i))
    return pl.pallas_call(
        functools.partial(norm_kernel, channels),
        grid=(width // WIDE,),
        in_specs=[column(tok), column(1)]
        + [pl.BlockSpec((8, tok), lambda i: (0, 0))] * len(squares),
        out_specs=column(tok),
        out_shape=jax.ShapeDtypeStruct((tok, width), BF16),
        compiler_params=pltpu.CompilerParams(vmem_limit_bytes=VMEM_BYTES),
        cost_estimate=pl.CostEstimate(
            flops=4 * tok * width, bytes_accessed=6 * tok * width, transcendentals=tok
        ),
        name="normed",
    )(gated, norm_gain, *squares)


def local(
    gate_in, key_in, value_in, long_filter, gate_short, key_short, value_short, skip_gain, norm_gain
):
    tok, width = value_in.shape
    blocks = lax.axis_size("seq")
    groups = lax.axis_size("ch")
    place = lax.axis_index("seq")
    position = jnp.full((1,), place, jnp.int32)
    halo = passed_along(
        jnp.concatenate([a[tok - HALO :] for a in (key_in, value_in, gate_in)], axis=0), "seq", 1
    )
    narrow = width // blocks // PARTS
    starts = [at * narrow * blocks for at in range(PARTS)]
    pack = lambda wants, start: packed(
        wants,
        ([long_filter] if "filter" in wants else [])
        + ([key_in, value_in, halo, key_short, value_short] if "product" in wants else []),
        (start, narrow, blocks),
        position,
    )
    far = blocks // NEAR
    sent = [pack(("filter",), starts[0]), pack(("product",), starts[0])]
    arrived = [[]]
    for parts in sent:
        arrived[0] += swap_far(swap_near(parts))
    for start in starts[1:]:
        parts = pack(("filter", "product"), start)
        arrived[0][:far], parts = lax.optimization_barrier((arrived[0][:far], parts))
        arrived[-1], lines = lax.optimization_barrier((arrived[-1], swap_near(parts)))
        arrived.append(swap_far(lines))
    mixed = []
    for start, arrays in zip(starts, arrived):
        skip = lax.dynamic_slice_in_dim(skip_gain, start + place * narrow, narrow, 0)
        skip = jnp.broadcast_to(skip[:, None], (narrow, LANES))
        mixed.append(swap_back(long_conv(arrays, skip, blocks, position)))
    gated = None
    for start, part in zip(starts, mixed):
        gated = gated_of(gate_in, halo, gate_short, part, start, gated, position)
    gated, squares = gated
    sums = [squares]
    for by in range(1, groups):
        sums.append(lax.ppermute(squares, "ch", [(i, (i + by) % groups) for i in range(groups)]))
    return normed(gated, sums, norm_gain[None, :], width * groups)


def solution(mesh):
    return jax.shard_map(
        local,
        mesh=mesh,
        in_specs=(
            P("seq", "ch"),
            P("seq", "ch"),
            P("seq", "ch"),
            P("seq", "ch"),
            P(None, "ch"),
            P(None, "ch"),
            P(None, "ch"),
            P("ch"),
            P("ch"),
        ),
        out_specs=P("seq", "ch"),
        check_vma=False,
    )
```

```python
import functools

import jax
import jax.numpy as jnp
from jax import lax
from jax.experimental import pallas as pl
from jax.experimental.pallas import tpu as pltpu
from jax.sharding import PartitionSpec as P

LANES = 128
FINE = 32
GROUP = 4
HALO = 16
WIDE = 512
PARTS = 2
NEAR = 4
VMEM_BYTES = 20 * 1024 * 1024
BRIEF = pl.CostEstimate(flops=1000, bytes_accessed=1000, transcendentals=0)
F32 = jnp.float32
BF16 = jnp.bfloat16


def passed_along(array, axis, by):
    size = lax.axis_size(axis)
    pairs = [(i, i + by) for i in range(size) if 0 <= i + by < size]
    return lax.ppermute(array, axis, pairs)


def short_conv(rows, prev, taps):
    last = prev[HALO - 1 : HALO]
    before = prev[HALO - 2 : HALO - 1]
    at = lax.broadcasted_iota(jnp.int32, rows.shape, 0)
    one = jnp.where(at == 0, last, pltpu.roll(rows, 1, 0))
    two = jnp.where(at == 0, before, jnp.where(at == 1, last, pltpu.roll(rows, 2, 0)))
    return taps[0:1] * rows + taps[1:2] * one + taps[2:3] * two


def pack_kernel(wants, at_ref, *refs):
    arrays = len(wants) + 4 * ("product" in wants)
    refs, outs, held = list(refs[:arrays]), refs[arrays:-1], refs[-1]
    _, _, narrow, tok = held.shape
    near = outs[0].shape[0]
    count = WIDE // narrow
    step = pl.program_id(0)
    for at, want in enumerate(wants):
        if want == "filter":
            rows = refs.pop(0)[...].astype(F32)
        else:
            key, value, halo, key_taps, value_taps = [refs.pop(0)[...] for _ in range(5)]
            halo = halo.astype(F32)
            rows = short_conv(key.astype(F32), halo[:HALO], key_taps)
            rows *= short_conv(value.astype(F32), halo[HALO : 2 * HALO], value_taps)
        held[pl.ds(step * count, count), at] = rows.T.astype(BF16).reshape(count, narrow, tok)

    @pl.when(step == pl.num_programs(0) - 1)
    def _():
        for j, out_ref in enumerate(outs):
            for i in range(near):
                out_ref[i] = held[at_ref[0] ^ (near * j + i)]


def packed(wants, arrays, part, near, position):
    start, narrow, blocks = part
    tok = arrays[0].shape[0]
    first = start // WIDE
    shape = (near, len(wants), narrow, tok)
    return pl.pallas_call(
        functools.partial(pack_kernel, wants),
        grid_spec=pltpu.PrefetchScalarGridSpec(
            num_scalar_prefetch=1,
            grid=(blocks * narrow // WIDE,),
            in_specs=[
                pl.BlockSpec((array.shape[0], WIDE), lambda i, at: (0, first + i))
                for array in arrays
            ],
            out_specs=[pl.BlockSpec(shape, lambda i, at: (0, 0, 0, 0))] * (blocks // near),
            scratch_shapes=[pltpu.VMEM((blocks,) + shape[1:], BF16)],
        ),
        out_shape=[jax.ShapeDtypeStruct(shape, BF16)] * (blocks // near),
        compiler_params=pltpu.CompilerParams(vmem_limit_bytes=VMEM_BYTES),
        cost_estimate=BRIEF,
        name="pack_" + "_".join(wants),
    )(position, *arrays)


def tails_kernel(*refs):
    for at, ref in enumerate(refs[:-1]):
        refs[-1][at * HALO : (at + 1) * HALO, :] = ref[...]


def tails(arrays):
    tok, width = arrays[0].shape
    return pl.pallas_call(
        tails_kernel,
        grid=(1,),
        in_specs=[pl.BlockSpec((HALO, width), lambda i: (tok // HALO - 1, 0))] * len(arrays),
        out_specs=pl.BlockSpec((HALO * len(arrays), width), lambda i: (0, 0)),
        out_shape=jax.ShapeDtypeStruct((HALO * len(arrays), width), BF16),
        name="tails",
    )(*arrays)


def swapped(rows, by):
    size = lax.axis_size("seq")
    return lax.ppermute(rows, "seq", [(i, i ^ by) for i in range(size)])


def swap_far(lines):
    order = sorted(range(1, len(lines)), key=lambda j: j == 1)
    came = {j: swapped(lines[j], NEAR * j) for j in order}
    return [lines[0]] + [came[j] for j in range(1, len(lines))]


def swap_near(lines):
    parts = [jnp.stack([line[i] for line in lines]) for i in range(NEAR)]
    return [parts[0]] + [swapped(parts[i], i) for i in range(1, NEAR)]


def after(arrays, *others):
    tokens = [other[(slice(0, 1),) * other.ndim] for other in others]
    return lax.optimization_barrier((arrays, tokens))[0]


def delayed(rows, by):
    at = lax.broadcasted_iota(jnp.int32, rows.shape, 1)
    return jnp.where(at < by, 0.0, pltpu.roll(rows, by, 1))


def halves(first, second, upper):
    return (
        jnp.where(upper, first, pltpu.roll(second, 4, second.ndim - 2)),
        jnp.where(upper, pltpu.roll(first, 4, first.ndim - 2), second),
    )


def left_rows(pairs, turns):
    tok = pairs.shape[1]
    lane_of = lax.broadcasted_iota(jnp.int32, (turns * 8, LANES), 1) // FINE
    own = lane_of == lax.broadcasted_iota(jnp.int32, (turns * 8, LANES), 0) % GROUP
    columns = []
    for a in range(tok // LANES):
        piece = pairs[:, a * LANES : (a + 1) * LANES]
        moved = [piece] + [pltpu.roll(piece, FINE * d, 1) for d in range(1, 4)]
        picked = []
        for e in range(LANES // FINE):
            spread = moved[(3 - e) % 4]
            for c in range(3):
                spread = jnp.where(lane_of == c, moved[(c - e) % 4], spread)
            picked.append(jnp.where(own, spread, 0.0).reshape(turns, 1, 8, LANES))
        columns.append(jnp.concatenate(picked, axis=1).reshape(turns * 32, LANES).astype(BF16))
    return jnp.concatenate(columns, axis=1)


def conv_kernel(at_ref, skip_ref, *refs):
    refs, (filt, prod, base, left, total, held) = refs[:-6], refs[-6:]
    blocks, lanes, tok = prod.shape
    near = next(at for at, ref in enumerate(refs) if len(ref.shape) == 3)
    in_refs, out_refs = refs[:near], refs[near:]
    merged = in_refs[0].shape[1] == 2
    count = near if merged else near // 2
    filt_refs, prod_refs = in_refs[:count], in_refs[-count:]
    length = blocks * tok
    turns = blocks // 2
    units = lanes // 16

    for i, (filt_ref, prod_ref) in enumerate(zip(filt_refs, prod_refs)):
        for j in range(filt_ref.shape[0]):
            block = at_ref[0] ^ (len(filt_refs) * j + i)
            lags = pl.ds(pl.multiple_of(block * tok, tok), tok)
            filt[:, lags] = filt_ref[j, 0].astype(F32)
            prod[block] = prod_ref[j, int(merged)].astype(F32)
    base[:, :, :LANES] = jnp.zeros((2, GROUP * FINE, LANES), BF16)

    def pairs_of(row, side):
        rows = prod[:, pl.ds(pl.multiple_of(row, 8), 8), :].reshape(turns, 2, 8, tok)
        upper = lax.broadcasted_iota(jnp.int32, (turns, 8, tok), 1) < 4
        return halves(rows[:, 0], rows[:, 1], upper)[side].reshape(turns * 8, tok)

    def build_left(row, side):
        left[side] = left_rows(pairs_of(row, side), turns)

    def build_base(row, side, c, pair):
        line = jnp.broadcast_to(filt[pl.ds(row + side * GROUP + c, 1), :], (8, length))
        steps = []
        for a in (2 * pair, 2 * pair + 1):
            shifted = pltpu.roll(line, 8 * a, 1, stride=1, stride_axis=0)
            late = lax.broadcasted_iota(
                jnp.int32, (8, LANES), 1
            ) >= 8 * a + lax.broadcasted_iota(jnp.int32, (8, LANES), 0)
            steps.append(
                jnp.concatenate(
                    [jnp.where(late, shifted[:, :LANES], 0.0), shifted[:, LANES:]], axis=1
                )
            )
        at = c * FINE + 16 * pair
        base[side, at : at + 16, LANES:] = jnp.concatenate(steps, axis=0).astype(BF16)

    jobs = [(c, pair) for c in range(GROUP) for pair in range(FINE // 16)]

    def multiply(side, k):
        start = k * tok
        right = jnp.concatenate(
            [
                base[side, :, LANES + start : LANES + start + tok],
                base[side, :, start : start + tok],
            ],
            axis=0,
        )
        count = turns - k // 2
        out = jnp.dot(left[side, : 32 * count], right, preferred_element_type=F32)
        for m in range(count):
            at = slice(start + 2 * tok * m, start + 2 * tok * m + tok)
            piece = out[32 * m : 32 * m + 32]
            if k < 2:
                total[side, :, at] = piece
            else:
                total[side, :, at] += piece

    def summed(side):
        run = total[side, 24:32]
        for e in (2, 1, 0):
            run = total[side, 8 * e : 8 * e + 8] + delayed(run, FINE)
        return run

    build_left(0, 0)
    for job in jobs:
        build_base(0, 0, *job)

    def unit(index, carry):
        done = []
        for part in range(2):
            row = index * 16 + 8 * part
            sums = []
            for side in range(2):
                if side == 0:
                    after = row
                elif part == 0:
                    after = row + 8
                else:
                    after = jnp.minimum(row + 8, lanes - 8)
                build_left(after, 1 - side)
                for k in range(blocks):
                    for at, job in enumerate(jobs):
                        if at * blocks // len(jobs) == k:
                            build_base(after, 1 - side, *job)
                    multiply(side, k)
                sums.append(summed(side))
            upper = lax.broadcasted_iota(jnp.int32, (8, length), 0) < 4
            even, odd = halves(sums[0], sums[1], upper)
            conv = even + jnp.concatenate(
                [jnp.zeros((8, tok), F32), odd[:, : length - tok]], axis=1
            )
            here = pl.ds(pl.multiple_of(row, 8), 8)
            skip = jnp.concatenate([skip_ref[here, :]] * (tok // LANES), axis=1)
            done.append(
                [conv[:, h * tok : (h + 1) * tok] + skip * prod[h, here, :] for h in range(blocks)]
            )
        for h in range(blocks):
            held[h, pl.ds(pl.multiple_of(index * 16, 16), 16), :] = jnp.concatenate(
                [done[0][h], done[1][h]], axis=0
            ).astype(BF16)
        return carry

    lax.fori_loop(0, units, unit, 0)
    for j, out_ref in enumerate(out_refs):
        for i in range(out_ref.shape[0]):
            out_ref[i] = held[at_ref[0] ^ (out_ref.shape[0] * j + i)]


def long_conv(arrays, skip_rows, blocks, near, position, cost=BRIEF):
    _, _, lanes, tok = arrays[0].shape
    length = blocks * tok
    whole = lambda array: pl.BlockSpec(array.shape, lambda i, at: (0,) * len(array.shape))
    out_shape = [jax.ShapeDtypeStruct((near, lanes, tok), BF16)] * (blocks // near)
    return pl.pallas_call(
        conv_kernel,
        grid_spec=pltpu.PrefetchScalarGridSpec(
            num_scalar_prefetch=1,
            grid=(1,),
            in_specs=[whole(array) for array in (skip_rows, *arrays)],
            out_specs=[whole(array) for array in out_shape],
            scratch_shapes=[
                pltpu.VMEM((lanes, length), F32),
                pltpu.VMEM((blocks, lanes, tok), F32),
                pltpu.VMEM((2, GROUP * FINE, LANES + length), BF16),
                pltpu.VMEM((2, 16 * blocks, 2 * LANES), BF16),
                pltpu.VMEM((2, 32, length), F32),
                pltpu.VMEM((blocks, lanes, tok), BF16),
            ],
        ),
        out_shape=out_shape,
        compiler_params=pltpu.CompilerParams(vmem_limit_bytes=VMEM_BYTES),
        cost_estimate=cost,
        name="long_conv",
    )(position, skip_rows, *arrays)


def gated_kernel(at_ref, gate_ref, halo_ref, taps_ref, *refs):
    held = refs[-1]
    blocks, narrow, tok = held.shape
    near = blocks // refs[0].shape[0]
    mixed_refs, refs = refs[:near], refs[near:-1]
    gated_ref, squares_ref = refs[-2:]
    count = WIDE // narrow
    step = pl.program_id(0)

    @pl.when(step == 0)
    def _():
        for i, mixed_ref in enumerate(mixed_refs):
            for j in range(mixed_ref.shape[0]):
                held[at_ref[0] ^ (near * j + i)] = mixed_ref[j]

    halo = halo_ref[...].astype(F32)
    gate = short_conv(gate_ref[...].astype(F32), halo[2 * HALO :], taps_ref[...])
    mixed = held[pl.ds(step * count, count)].reshape(WIDE, tok)
    gated = gate * mixed.astype(F32).T
    gated_ref[...] = gated
    squares = gated * gated
    part = squares[:, :LANES]
    for at in range(LANES, WIDE, LANES):
        part = part + squares[:, at : at + LANES]
    turned = jnp.sum(part.T.reshape(LANES // 8, 8, part.shape[0]), axis=0)

    @pl.when(step == 0)
    def _():
        squares_ref[...] = refs[0][...] + turned if len(refs) > 2 else turned

    @pl.when(step > 0)
    def _():
        squares_ref[...] += turned


def gated_of(gate_in, halo, gate_short, mixed, start, before, position):
    tok, full = gate_in.shape
    far, narrow, _ = mixed[0].shape
    near = len(mixed)
    width = near * far * narrow
    first = start // WIDE
    column = lambda rows: pl.BlockSpec((rows, WIDE), lambda i, at: (0, first + i))
    sums = pl.BlockSpec((8, tok), lambda i, at: (0, 0))
    more = [] if before is None else [sums, pl.BlockSpec(memory_space=pl.ANY)]
    return pl.pallas_call(
        gated_kernel,
        grid_spec=pltpu.PrefetchScalarGridSpec(
            num_scalar_prefetch=1,
            grid=(width // WIDE,),
            in_specs=[column(tok), column(3 * HALO), column(3)]
            + [pl.BlockSpec(mixed[0].shape, lambda i, at: (0, 0, 0))] * near
            + more,
            out_specs=[column(tok), sums],
            scratch_shapes=[pltpu.VMEM((near * far, narrow, tok), BF16)],
        ),
        out_shape=[
            jax.ShapeDtypeStruct((tok, full), F32),
            jax.ShapeDtypeStruct((8, tok), F32),
        ],
        input_output_aliases={5 + near: 0} if more else {},
        compiler_params=pltpu.CompilerParams(vmem_limit_bytes=VMEM_BYTES),
        cost_estimate=BRIEF,
        name="gated_squares",
    )(
        position,
        gate_in,
        halo,
        gate_short,
        *mixed,
        *(() if before is None else (before[1], before[0])),
    )


def norm_kernel(channels, gated_ref, gain_ref, *refs):
    sums, out_ref = refs[:-1], refs[-1]
    total = sums[0][...]
    for other in sums[1:]:
        total = total + other[...]
    total = jnp.sum(total, axis=0, keepdims=True)
    scale = lax.rsqrt(total / channels + 1e-06)
    scale = jnp.broadcast_to(scale, (LANES, scale.shape[1])).T
    scale = jnp.concatenate([scale] * (WIDE // LANES), axis=1)
    out_ref[...] = (gated_ref[...] * gain_ref[...] * scale).astype(BF16)


def normed(gated, squares, norm_gain, channels):
    tok, width = gated.shape
    column = lambda rows: pl.BlockSpec((rows, WIDE), lambda i: (0, i))
    return pl.pallas_call(
        functools.partial(norm_kernel, channels),
        grid=(width // WIDE,),
        in_specs=[column(tok), column(1)]
        + [pl.BlockSpec((8, tok), lambda i: (0, 0))] * len(squares),
        out_specs=column(tok),
        out_shape=jax.ShapeDtypeStruct((tok, width), BF16),
        compiler_params=pltpu.CompilerParams(vmem_limit_bytes=VMEM_BYTES),
        cost_estimate=BRIEF,
        name="normed",
    )(gated, norm_gain, *squares)


def local(
    gate_in, key_in, value_in, long_filter, gate_short, key_short, value_short, skip_gain, norm_gain
):
    tok, width = value_in.shape
    blocks = lax.axis_size("seq")
    groups = lax.axis_size("ch")
    place = lax.axis_index("seq")
    position = jnp.full((1,), place, jnp.int32)
    narrow = width // blocks // PARTS
    starts = [at * narrow * blocks for at in range(PARTS)]
    exchange = lambda rows: lax.all_to_all(rows, "seq", split_axis=0, concat_axis=0, tiled=True)
    natural = jnp.zeros((1,), jnp.int32)
    pack = lambda wants, start, near, origin: packed(
        wants,
        ([long_filter] if "filter" in wants else [])
        + ([key_in, value_in, halo, key_short, value_short] if "product" in wants else []),
        (start, narrow, blocks),
        near,
        origin,
    )

    def skip_of(start):
        skip = lax.dynamic_slice_in_dim(skip_gain, start + place * narrow, narrow, 0)
        return jnp.broadcast_to(skip[:, None], (narrow, LANES))

    lines = pack(("filter",), starts[0], NEAR, position)
    halo = passed_along(tails((key_in, value_in, gate_in)), "seq", 1)
    came = swap_far(pack(("product",), starts[0], NEAR, position))
    filters = swap_near(after(swap_far(lines), came[2]))
    products = swap_near(came)
    second = pack(("filter", "product"), starts[1], blocks, natural)[0]
    second = exchange(after(second, came[2]))
    lines = long_conv(filters + products, skip_of(starts[0]), blocks, NEAR, position)
    lines = swap_far(after(lines, second))
    cost = pl.CostEstimate(
        flops=2 * width * tok * tok * blocks, bytes_accessed=6 * tok * width, transcendentals=0
    )
    last = long_conv([second], skip_of(starts[1]), blocks, blocks, natural, cost)[0]
    lines, last = lax.optimization_barrier((lines, last))
    last = exchange(last)
    gated = gated_of(gate_in, halo, gate_short, swap_near(lines), starts[0], None, position)
    gated = gated_of(gate_in, halo, gate_short, [last], starts[1], gated, natural)
    gated, squares = gated
    sums = [squares]
    for by in range(1, groups):
        sums.append(lax.ppermute(squares, "ch", [(i, (i + by) % groups) for i in range(groups)]))
    return normed(gated, sums, norm_gain[None, :], width * groups)


def solution(mesh):
    return jax.shard_map(
        local,
        mesh=mesh,
        in_specs=(
            P("seq", "ch"),
            P("seq", "ch"),
            P("seq", "ch"),
            P("seq", "ch"),
            P(None, "ch"),
            P(None, "ch"),
            P(None, "ch"),
            P("ch"),
            P("ch"),
        ),
        out_specs=P("seq", "ch"),
        check_vma=False,
    )
```

```python
import functools

import jax
import jax.numpy as jnp
from jax import lax
from jax.experimental import pallas as pl
from jax.experimental.pallas import tpu as pltpu
from jax.sharding import PartitionSpec as P

LANES = 128
FINE = 32
GROUP = 4
HALO = 16
WIDE = 512
PARTS = 2
NEAR = 4
VMEM_BYTES = 20 * 1024 * 1024
BRIEF = pl.CostEstimate(flops=1000, bytes_accessed=1000, transcendentals=0)
DONE = jax.ShapeDtypeStruct((8, 128), jnp.float32)
F32 = jnp.float32
BF16 = jnp.bfloat16


def corner(array):
    block = (1,) * (len(array.shape) - 2) + (8 if array.dtype == F32 else 16, LANES)
    return pl.BlockSpec(block, lambda *at: (0,) * len(block))


def passed_along(array, axis, by):
    size = lax.axis_size(axis)
    pairs = [(i, i + by) for i in range(size) if 0 <= i + by < size]
    return lax.ppermute(array, axis, pairs)


def short_conv(rows, prev, taps):
    last = prev[HALO - 1 : HALO]
    before = prev[HALO - 2 : HALO - 1]
    at = lax.broadcasted_iota(jnp.int32, rows.shape, 0)
    one = jnp.where(at == 0, last, pltpu.roll(rows, 1, 0))
    two = jnp.where(at == 0, before, jnp.where(at == 1, last, pltpu.roll(rows, 2, 0)))
    return taps[0:1] * rows + taps[1:2] * one + taps[2:3] * two


def pack_kernel(wants, waits, at_ref, *refs):
    arrays = len(wants) + 4 * ("product" in wants)
    refs, outs, done_ref, held = list(refs[:arrays]), refs[arrays + waits : -2], refs[-2], refs[-1]
    done_ref[...] = jnp.zeros_like(done_ref)
    _, _, narrow, tok = held.shape
    count = WIDE // narrow
    step = pl.program_id(0)
    for at, want in enumerate(wants):
        if want == "filter":
            rows = refs.pop(0)[...].astype(F32)
        else:
            key, value, halo, key_taps, value_taps = [refs.pop(0)[...] for _ in range(5)]
            halo = halo.astype(F32)
            rows = short_conv(key.astype(F32), halo[:HALO], key_taps)
            rows *= short_conv(value.astype(F32), halo[HALO : 2 * HALO], value_taps)
        held[pl.ds(step * count, count), at] = rows.T.astype(BF16).reshape(count, narrow, tok)

    @pl.when(step == pl.num_programs(0) - 1)
    def _():
        for i, out_ref in enumerate(outs):
            for j in range(out_ref.shape[0]):
                out_ref[j] = held[at_ref[0] ^ (len(outs) * j + i)]


def packed(wants, arrays, later, part, near, position):
    start, narrow, blocks = part
    tok = arrays[0].shape[0]
    first = start // WIDE
    shape = (blocks // near, len(wants), narrow, tok)
    return pl.pallas_call(
        functools.partial(pack_kernel, wants, len(later)),
        grid_spec=pltpu.PrefetchScalarGridSpec(
            num_scalar_prefetch=1,
            grid=(blocks * narrow // WIDE,),
            in_specs=[
                pl.BlockSpec((array.shape[0], WIDE), lambda i, at: (0, first + i))
                for array in arrays
            ]
            + [corner(array) for array in later],
            out_specs=[pl.BlockSpec(shape, lambda i, at: (0, 0, 0, 0))] * near
            + [pl.BlockSpec(DONE.shape, lambda i, at: (0, 0))],
            scratch_shapes=[pltpu.VMEM((blocks,) + shape[1:], BF16)],
        ),
        out_shape=[jax.ShapeDtypeStruct(shape, BF16)] * near + [DONE],
        compiler_params=pltpu.CompilerParams(vmem_limit_bytes=VMEM_BYTES),
        cost_estimate=BRIEF,
        name="pack_" + "_".join(wants),
    )(position, *arrays, *later)


def tails_kernel(*refs):
    for at, ref in enumerate(refs[:-1]):
        refs[-1][at * HALO : (at + 1) * HALO, :] = ref[...]


def tails(arrays):
    tok, width = arrays[0].shape
    return pl.pallas_call(
        tails_kernel,
        grid=(1,),
        in_specs=[pl.BlockSpec((HALO, width), lambda i: (tok // HALO - 1, 0))] * len(arrays),
        out_specs=pl.BlockSpec((HALO * len(arrays), width), lambda i: (0, 0)),
        out_shape=jax.ShapeDtypeStruct((HALO * len(arrays), width), BF16),
        name="tails",
    )(*arrays)


def swapped(rows, by):
    size = lax.axis_size("seq")
    return lax.ppermute(rows, "seq", [(i, i ^ by) for i in range(size)])


def swap_far(lines):
    order = sorted(range(1, len(lines)), key=lambda j: j == 1)
    came = {j: swapped(lines[j], NEAR * j) for j in order}
    return [lines[0]] + [came[j] for j in range(1, len(lines))]


def plane_first(parts):
    return [parts[0]] + [swapped(parts[i], i) for i in range(1, NEAR)]


def regroup_kernel(count, *refs):
    for i, out_ref in enumerate(refs[-count:]):
        for j in range(out_ref.shape[0]):
            out_ref[j] = refs[j][i]


def regroup(lines, later):
    whole = lambda array: pl.BlockSpec(array.shape, lambda i: (0,) * len(array.shape))
    count = lines[0].shape[0]
    out_shape = [jax.ShapeDtypeStruct((len(lines),) + lines[0].shape[1:], BF16)] * count
    return pl.pallas_call(
        functools.partial(regroup_kernel, count),
        grid=(1,),
        in_specs=[whole(line) for line in lines] + [corner(array) for array in later],
        out_specs=[whole(array) for array in out_shape],
        out_shape=out_shape,
        compiler_params=pltpu.CompilerParams(vmem_limit_bytes=VMEM_BYTES),
        cost_estimate=BRIEF,
        name="regroup",
    )(*lines, *later)


def swap_near(lines, later):
    return plane_first(regroup(lines, later))


def delayed(rows, by):
    at = lax.broadcasted_iota(jnp.int32, rows.shape, 1)
    return jnp.where(at < by, 0.0, pltpu.roll(rows, by, 1))


def halves(first, second, upper):
    return (
        jnp.where(upper, first, pltpu.roll(second, 4, second.ndim - 2)),
        jnp.where(upper, pltpu.roll(first, 4, first.ndim - 2), second),
    )


def left_rows(pairs, turns):
    tok = pairs.shape[1]
    lane_of = lax.broadcasted_iota(jnp.int32, (turns * 8, LANES), 1) // FINE
    own = lane_of == lax.broadcasted_iota(jnp.int32, (turns * 8, LANES), 0) % GROUP
    columns = []
    for a in range(tok // LANES):
        piece = pairs[:, a * LANES : (a + 1) * LANES]
        moved = [piece] + [pltpu.roll(piece, FINE * d, 1) for d in range(1, 4)]
        picked = []
        for e in range(LANES // FINE):
            spread = moved[(3 - e) % 4]
            for c in range(3):
                spread = jnp.where(lane_of == c, moved[(c - e) % 4], spread)
            picked.append(jnp.where(own, spread, 0.0).reshape(turns, 1, 8, LANES))
        columns.append(jnp.concatenate(picked, axis=1).reshape(turns * 32, LANES).astype(BF16))
    return jnp.concatenate(columns, axis=1)


def conv_kernel(at_ref, skip_ref, later_ref, *refs):
    refs, (done_ref, filt, prod, base, left, total, held) = refs[:-7], refs[-7:]
    done_ref[...] = jnp.zeros_like(done_ref)
    blocks, lanes, tok = prod.shape
    near = next(at for at, ref in enumerate(refs) if len(ref.shape) == 3)
    in_refs, out_refs = refs[:near], refs[near:]
    merged = in_refs[0].shape[1] == 2
    count = near if merged else near // 2
    filt_refs, prod_refs = in_refs[:count], in_refs[-count:]
    length = blocks * tok
    turns = blocks // 2
    units = lanes // 16

    for j, (filt_ref, prod_ref) in enumerate(zip(filt_refs, prod_refs)):
        for i in range(filt_ref.shape[0]):
            block = at_ref[0] ^ (filt_ref.shape[0] * j + i)
            lags = pl.ds(pl.multiple_of(block * tok, tok), tok)
            filt[:, lags] = filt_ref[i, 0].astype(F32)
            prod[block] = prod_ref[i, int(merged)].astype(F32)
    base[:, :, :LANES] = jnp.zeros((2, GROUP * FINE, LANES), BF16)

    def pairs_of(row, side):
        rows = prod[:, pl.ds(pl.multiple_of(row, 8), 8), :].reshape(turns, 2, 8, tok)
        upper = lax.broadcasted_iota(jnp.int32, (turns, 8, tok), 1) < 4
        return halves(rows[:, 0], rows[:, 1], upper)[side].reshape(turns * 8, tok)

    def build_left(row, side):
        left[side] = left_rows(pairs_of(row, side), turns)

    def build_base(row, side, c, pair):
        line = jnp.broadcast_to(filt[pl.ds(row + side * GROUP + c, 1), :], (8, length))
        steps = []
        for a in (2 * pair, 2 * pair + 1):
            shifted = pltpu.roll(line, 8 * a, 1, stride=1, stride_axis=0)
            late = lax.broadcasted_iota(
                jnp.int32, (8, LANES), 1
            ) >= 8 * a + lax.broadcasted_iota(jnp.int32, (8, LANES), 0)
            steps.append(
                jnp.concatenate(
                    [jnp.where(late, shifted[:, :LANES], 0.0), shifted[:, LANES:]], axis=1
                )
            )
        at = c * FINE + 16 * pair
        base[side, at : at + 16, LANES:] = jnp.concatenate(steps, axis=0).astype(BF16)

    jobs = [(c, pair) for c in range(GROUP) for pair in range(FINE // 16)]

    def multiply(side, k):
        start = k * tok
        right = jnp.concatenate(
            [
                base[side, :, LANES + start : LANES + start + tok],
                base[side, :, start : start + tok],
            ],
            axis=0,
        )
        count = turns - k // 2
        out = jnp.dot(left[side, : 32 * count], right, preferred_element_type=F32)
        for m in range(count):
            at = slice(start + 2 * tok * m, start + 2 * tok * m + tok)
            piece = out[32 * m : 32 * m + 32]
            if k < 2:
                total[side, :, at] = piece
            else:
                total[side, :, at] += piece

    def summed(side):
        run = total[side, 24:32]
        for e in (2, 1, 0):
            run = total[side, 8 * e : 8 * e + 8] + delayed(run, FINE)
        return run

    build_left(0, 0)
    for job in jobs:
        build_base(0, 0, *job)

    def unit(index, carry):
        done = []
        for part in range(2):
            row = index * 16 + 8 * part
            sums = []
            for side in range(2):
                if side == 0:
                    after = row
                elif part == 0:
                    after = row + 8
                else:
                    after = jnp.minimum(row + 8, lanes - 8)
                build_left(after, 1 - side)
                for k in range(blocks):
                    for at, job in enumerate(jobs):
                        if at * blocks // len(jobs) == k:
                            build_base(after, 1 - side, *job)
                    multiply(side, k)
                sums.append(summed(side))
            upper = lax.broadcasted_iota(jnp.int32, (8, length), 0) < 4
            even, odd = halves(sums[0], sums[1], upper)
            conv = even + jnp.concatenate(
                [jnp.zeros((8, tok), F32), odd[:, : length - tok]], axis=1
            )
            here = pl.ds(pl.multiple_of(row, 8), 8)
            skip = jnp.concatenate([skip_ref[here, :]] * (tok // LANES), axis=1)
            done.append(
                [conv[:, h * tok : (h + 1) * tok] + skip * prod[h, here, :] for h in range(blocks)]
            )
        for h in range(blocks):
            held[h, pl.ds(pl.multiple_of(index * 16, 16), 16), :] = jnp.concatenate(
                [done[0][h], done[1][h]], axis=0
            ).astype(BF16)
        return carry

    lax.fori_loop(0, units, unit, 0)
    for j, out_ref in enumerate(out_refs):
        for i in range(out_ref.shape[0]):
            out_ref[i] = held[at_ref[0] ^ (out_ref.shape[0] * j + i)]


def long_conv(arrays, skip_rows, later, blocks, near, position, cost=BRIEF):
    _, _, lanes, tok = arrays[0].shape
    length = blocks * tok
    whole = lambda array: pl.BlockSpec(array.shape, lambda i, at: (0,) * len(array.shape))
    out_shape = [jax.ShapeDtypeStruct((near, lanes, tok), BF16)] * (blocks // near) + [DONE]
    return pl.pallas_call(
        conv_kernel,
        grid_spec=pltpu.PrefetchScalarGridSpec(
            num_scalar_prefetch=1,
            grid=(1,),
            in_specs=[whole(skip_rows), corner(later)] + [whole(array) for array in arrays],
            out_specs=[whole(array) for array in out_shape],
            scratch_shapes=[
                pltpu.VMEM((lanes, length), F32),
                pltpu.VMEM((blocks, lanes, tok), F32),
                pltpu.VMEM((2, GROUP * FINE, LANES + length), BF16),
                pltpu.VMEM((2, 16 * blocks, 2 * LANES), BF16),
                pltpu.VMEM((2, 32, length), F32),
                pltpu.VMEM((blocks, lanes, tok), BF16),
            ],
        ),
        out_shape=out_shape,
        compiler_params=pltpu.CompilerParams(vmem_limit_bytes=VMEM_BYTES),
        cost_estimate=cost,
        name="long_conv",
    )(position, skip_rows, later, *arrays)


def gated_kernel(at_ref, gate_ref, halo_ref, taps_ref, *refs):
    held = refs[-1]
    blocks, narrow, tok = held.shape
    near = blocks // refs[0].shape[0]
    mixed_refs, refs = refs[:near], refs[near:-1]
    gated_ref, squares_ref = refs[-2:]
    count = WIDE // narrow
    step = pl.program_id(0)

    @pl.when(step == 0)
    def _():
        for i, mixed_ref in enumerate(mixed_refs):
            for j in range(mixed_ref.shape[0]):
                held[at_ref[0] ^ (near * j + i)] = mixed_ref[j]

    halo = halo_ref[...].astype(F32)
    gate = short_conv(gate_ref[...].astype(F32), halo[2 * HALO :], taps_ref[...])
    mixed = held[pl.ds(step * count, count)].reshape(WIDE, tok)
    gated = gate * mixed.astype(F32).T
    gated_ref[...] = gated
    squares = gated * gated
    part = squares[:, :LANES]
    for at in range(LANES, WIDE, LANES):
        part = part + squares[:, at : at + LANES]
    turned = jnp.sum(part.T.reshape(LANES // 8, 8, part.shape[0]), axis=0)

    @pl.when(step == 0)
    def _():
        squares_ref[...] = refs[0][...] + turned if len(refs) > 2 else turned

    @pl.when(step > 0)
    def _():
        squares_ref[...] += turned


def gated_of(gate_in, halo, gate_short, mixed, start, before, position):
    tok, full = gate_in.shape
    far, narrow, _ = mixed[0].shape
    near = len(mixed)
    width = near * far * narrow
    first = start // WIDE
    column = lambda rows: pl.BlockSpec((rows, WIDE), lambda i, at: (0, first + i))
    sums = pl.BlockSpec((8, tok), lambda i, at: (0, 0))
    more = [] if before is None else [sums, pl.BlockSpec(memory_space=pl.ANY)]
    return pl.pallas_call(
        gated_kernel,
        grid_spec=pltpu.PrefetchScalarGridSpec(
            num_scalar_prefetch=1,
            grid=(width // WIDE,),
            in_specs=[column(tok), column(3 * HALO), column(3)]
            + [pl.BlockSpec(mixed[0].shape, lambda i, at: (0, 0, 0))] * near
            + more,
            out_specs=[column(tok), sums],
            scratch_shapes=[pltpu.VMEM((near * far, narrow, tok), BF16)],
        ),
        out_shape=[
            jax.ShapeDtypeStruct((tok, full), F32),
            jax.ShapeDtypeStruct((8, tok), F32),
        ],
        input_output_aliases={5 + near: 0} if more else {},
        compiler_params=pltpu.CompilerParams(vmem_limit_bytes=VMEM_BYTES),
        cost_estimate=BRIEF,
        name="gated_squares",
    )(
        position,
        gate_in,
        halo,
        gate_short,
        *mixed,
        *(() if before is None else (before[1], before[0])),
    )


def norm_kernel(channels, gated_ref, gain_ref, *refs):
    sums, out_ref = refs[:-1], refs[-1]
    total = sums[0][...]
    for other in sums[1:]:
        total = total + other[...]
    total = jnp.sum(total, axis=0, keepdims=True)
    scale = lax.rsqrt(total / channels + 1e-06)
    scale = jnp.broadcast_to(scale, (LANES, scale.shape[1])).T
    scale = jnp.concatenate([scale] * (WIDE // LANES), axis=1)
    out_ref[...] = (gated_ref[...] * gain_ref[...] * scale).astype(BF16)


def normed(gated, squares, norm_gain, channels):
    tok, width = gated.shape
    column = lambda rows: pl.BlockSpec((rows, WIDE), lambda i: (0, i))
    return pl.pallas_call(
        functools.partial(norm_kernel, channels),
        grid=(width // WIDE,),
        in_specs=[column(tok), column(1)]
        + [pl.BlockSpec((8, tok), lambda i: (0, 0))] * len(squares),
        out_specs=column(tok),
        out_shape=jax.ShapeDtypeStruct((tok, width), BF16),
        compiler_params=pltpu.CompilerParams(vmem_limit_bytes=VMEM_BYTES),
        cost_estimate=BRIEF,
        name="normed",
    )(gated, norm_gain, *squares)


def local(
    gate_in, key_in, value_in, long_filter, gate_short, key_short, value_short, skip_gain, norm_gain
):
    tok, width = value_in.shape
    blocks = lax.axis_size("seq")
    groups = lax.axis_size("ch")
    place = lax.axis_index("seq")
    position = jnp.full((1,), place, jnp.int32)
    narrow = width // blocks // PARTS
    starts = [at * narrow * blocks for at in range(PARTS)]
    exchange = lambda rows: lax.all_to_all(rows, "seq", split_axis=0, concat_axis=0, tiled=True)
    natural = jnp.zeros((1,), jnp.int32)
    pack = lambda wants, start, near, origin, later: packed(
        wants,
        ([long_filter] if "filter" in wants else [])
        + ([key_in, value_in, halo, key_short, value_short] if "product" in wants else []),
        later,
        (start, narrow, blocks),
        near,
        origin,
    )

    def skip_of(start):
        skip = lax.dynamic_slice_in_dim(skip_gain, start + place * narrow, narrow, 0)
        return jnp.broadcast_to(skip[:, None], (narrow, LANES))

    halo = passed_along(tails((key_in, value_in, gate_in)), "seq", 1)
    *lines, _ = pack(("filter",), starts[0], NEAR, position, [])
    filters = swap_far(regroup(plane_first(lines), []))
    *product, _ = pack(("product",), starts[0], NEAR, position, [])
    product = plane_first(product)
    products = swap_far(regroup(product, filters[1:]))
    second, done = pack(("filter", "product"), starts[1], 1, natural, filters[1:2] + products[1:])
    second = exchange(second)
    *lines, ended = long_conv(filters + products, skip_of(starts[0]), done, blocks, NEAR, position)
    lines, second = lax.optimization_barrier((lines, second))
    lines = swap_far(lines)
    cost = pl.CostEstimate(
        flops=2 * width * tok * tok * blocks, bytes_accessed=6 * tok * width, transcendentals=0
    )
    last, done = long_conv([second], skip_of(starts[1]), ended, blocks, blocks, natural, cost)
    lines, last, done = lax.optimization_barrier((lines, last, done))
    first = swap_near(lines, [done])
    last = exchange(last)
    gated = gated_of(gate_in, halo, gate_short, first, starts[0], None, position)
    gated = gated_of(gate_in, halo, gate_short, [last], starts[1], gated, natural)
    gated, squares = gated
    sums = [squares]
    for by in range(1, groups):
        sums.append(lax.ppermute(squares, "ch", [(i, (i + by) % groups) for i in range(groups)]))
    return normed(gated, sums, norm_gain[None, :], width * groups)


def solution(mesh):
    return jax.shard_map(
        local,
        mesh=mesh,
        in_specs=(
            P("seq", "ch"),
            P("seq", "ch"),
            P("seq", "ch"),
            P("seq", "ch"),
            P(None, "ch"),
            P(None, "ch"),
            P(None, "ch"),
            P("ch"),
            P("ch"),
        ),
        out_specs=P("seq", "ch"),
        check_vma=False,
    )
```

```python
import functools

import jax
import jax.numpy as jnp
from jax import lax
from jax.experimental import pallas as pl
from jax.experimental.pallas import tpu as pltpu
from jax.sharding import PartitionSpec as P

LANES = 128
FINE = 32
GROUP = 4
HALO = 16
WIDE = 512
PARTS = 2
NEAR = 4
VMEM_BYTES = 20 * 1024 * 1024
BRIEF = pl.CostEstimate(flops=1000, bytes_accessed=1000, transcendentals=0)
DONE = jax.ShapeDtypeStruct((8, 128), jnp.float32)
F32 = jnp.float32
BF16 = jnp.bfloat16


def corner(array):
    block = (1,) * (len(array.shape) - 2) + (8 if array.dtype == F32 else 16, LANES)
    return pl.BlockSpec(block, lambda *at: (0,) * len(block))


def passed_along(array, axis, by):
    size = lax.axis_size(axis)
    pairs = [(i, i + by) for i in range(size) if 0 <= i + by < size]
    return lax.ppermute(array, axis, pairs)


def short_conv(rows, prev, taps):
    last = prev[HALO - 1 : HALO]
    before = prev[HALO - 2 : HALO - 1]
    at = lax.broadcasted_iota(jnp.int32, rows.shape, 0)
    one = jnp.where(at == 0, last, pltpu.roll(rows, 1, 0))
    two = jnp.where(at == 0, before, jnp.where(at == 1, last, pltpu.roll(rows, 2, 0)))
    return taps[0:1] * rows + taps[1:2] * one + taps[2:3] * two


def pack_kernel(wants, waits, at_ref, *refs):
    arrays = len(wants) + 4 * ("product" in wants)
    refs, outs, done_ref, held = list(refs[:arrays]), refs[arrays + waits : -2], refs[-2], refs[-1]
    done_ref[...] = jnp.zeros_like(done_ref)
    _, _, narrow, tok = held.shape
    near = outs[0].shape[0]
    count = WIDE // narrow
    step = pl.program_id(0)
    for at, want in enumerate(wants):
        if want == "filter":
            rows = refs.pop(0)[...].astype(F32)
        else:
            key, value, halo, key_taps, value_taps = [refs.pop(0)[...] for _ in range(5)]
            halo = halo.astype(F32)
            rows = short_conv(key.astype(F32), halo[:HALO], key_taps)
            rows *= short_conv(value.astype(F32), halo[HALO : 2 * HALO], value_taps)
        held[pl.ds(step * count, count), at] = rows.T.astype(BF16).reshape(count, narrow, tok)

    @pl.when(step == pl.num_programs(0) - 1)
    def _():
        for j, out_ref in enumerate(outs):
            for i in range(near):
                out_ref[i] = held[at_ref[0] ^ (near * j + i)]


def packed(wants, arrays, later, part, near, position):
    start, narrow, blocks = part
    tok = arrays[0].shape[0]
    first = start // WIDE
    shape = (near, len(wants), narrow, tok)
    return pl.pallas_call(
        functools.partial(pack_kernel, wants, len(later)),
        grid_spec=pltpu.PrefetchScalarGridSpec(
            num_scalar_prefetch=1,
            grid=(blocks * narrow // WIDE,),
            in_specs=[
                pl.BlockSpec((array.shape[0], WIDE), lambda i, at: (0, first + i))
                for array in arrays
            ]
            + [corner(array) for array in later],
            out_specs=[pl.BlockSpec(shape, lambda i, at: (0, 0, 0, 0))] * (blocks // near)
            + [pl.BlockSpec(DONE.shape, lambda i, at: (0, 0))],
            scratch_shapes=[pltpu.VMEM((blocks,) + shape[1:], BF16)],
        ),
        out_shape=[jax.ShapeDtypeStruct(shape, BF16)] * (blocks // near) + [DONE],
        compiler_params=pltpu.CompilerParams(vmem_limit_bytes=VMEM_BYTES),
        cost_estimate=BRIEF,
        name="pack_" + "_".join(wants),
    )(position, *arrays, *later)


def tails_kernel(*refs):
    for at, ref in enumerate(refs[:-1]):
        refs[-1][at * HALO : (at + 1) * HALO, :] = ref[...]


def tails(arrays):
    tok, width = arrays[0].shape
    return pl.pallas_call(
        tails_kernel,
        grid=(1,),
        in_specs=[pl.BlockSpec((HALO, width), lambda i: (tok // HALO - 1, 0))] * len(arrays),
        out_specs=pl.BlockSpec((HALO * len(arrays), width), lambda i: (0, 0)),
        out_shape=jax.ShapeDtypeStruct((HALO * len(arrays), width), BF16),
        name="tails",
    )(*arrays)


def swapped(rows, by):
    size = lax.axis_size("seq")
    return lax.ppermute(rows, "seq", [(i, i ^ by) for i in range(size)])


def swap_far(lines):
    order = sorted(range(1, len(lines)), key=lambda j: j == 1)
    came = {j: swapped(lines[j], NEAR * j) for j in order}
    return [lines[0]] + [came[j] for j in range(1, len(lines))]


def regroup_kernel(*refs):
    outs = refs[-NEAR:]
    for i, out_ref in enumerate(outs):
        for j in range(out_ref.shape[0]):
            out_ref[j] = refs[j][i]


def regroup(lines, later):
    whole = lambda array: pl.BlockSpec(array.shape, lambda i: (0,) * len(array.shape))
    out_shape = [jax.ShapeDtypeStruct((len(lines),) + lines[0].shape[1:], BF16)] * NEAR
    return pl.pallas_call(
        regroup_kernel,
        grid=(1,),
        in_specs=[whole(line) for line in lines] + [corner(later)],
        out_specs=[whole(array) for array in out_shape],
        out_shape=out_shape,
        compiler_params=pltpu.CompilerParams(vmem_limit_bytes=VMEM_BYTES),
        cost_estimate=BRIEF,
        name="regroup",
    )(*lines, later)


def swap_near(lines, later):
    parts = regroup(lines, later)
    return [parts[0]] + [swapped(parts[i], i) for i in range(1, NEAR)]


def delayed(rows, by):
    at = lax.broadcasted_iota(jnp.int32, rows.shape, 1)
    return jnp.where(at < by, 0.0, pltpu.roll(rows, by, 1))


def halves(first, second, upper):
    return (
        jnp.where(upper, first, pltpu.roll(second, 4, second.ndim - 2)),
        jnp.where(upper, pltpu.roll(first, 4, first.ndim - 2), second),
    )


def left_rows(pairs, turns):
    tok = pairs.shape[1]
    lane_of = lax.broadcasted_iota(jnp.int32, (turns * 8, LANES), 1) // FINE
    own = lane_of == lax.broadcasted_iota(jnp.int32, (turns * 8, LANES), 0) % GROUP
    columns = []
    for a in range(tok // LANES):
        piece = pairs[:, a * LANES : (a + 1) * LANES]
        moved = [piece] + [pltpu.roll(piece, FINE * d, 1) for d in range(1, 4)]
        picked = []
        for e in range(LANES // FINE):
            spread = moved[(3 - e) % 4]
            for c in range(3):
                spread = jnp.where(lane_of == c, moved[(c - e) % 4], spread)
            picked.append(jnp.where(own, spread, 0.0).reshape(turns, 1, 8, LANES))
        columns.append(jnp.concatenate(picked, axis=1).reshape(turns * 32, LANES).astype(BF16))
    return jnp.concatenate(columns, axis=1)


def conv_kernel(at_ref, skip_ref, later_ref, *refs):
    refs, (done_ref, filt, prod, base, left, total, held) = refs[:-7], refs[-7:]
    done_ref[...] = jnp.zeros_like(done_ref)
    blocks, lanes, tok = prod.shape
    near = next(at for at, ref in enumerate(refs) if len(ref.shape) == 3)
    in_refs, out_refs = refs[:near], refs[near:]
    merged = in_refs[0].shape[1] == 2
    count = near if merged else near // 2
    filt_refs, prod_refs = in_refs[:count], in_refs[-count:]
    length = blocks * tok
    turns = blocks // 2
    units = lanes // 16

    for i, (filt_ref, prod_ref) in enumerate(zip(filt_refs, prod_refs)):
        for j in range(filt_ref.shape[0]):
            block = at_ref[0] ^ (len(filt_refs) * j + i)
            lags = pl.ds(pl.multiple_of(block * tok, tok), tok)
            filt[:, lags] = filt_ref[j, 0].astype(F32)
            prod[block] = prod_ref[j, int(merged)].astype(F32)
    base[:, :, :LANES] = jnp.zeros((2, GROUP * FINE, LANES), BF16)

    def pairs_of(row, side):
        rows = prod[:, pl.ds(pl.multiple_of(row, 8), 8), :].reshape(turns, 2, 8, tok)
        upper = lax.broadcasted_iota(jnp.int32, (turns, 8, tok), 1) < 4
        return halves(rows[:, 0], rows[:, 1], upper)[side].reshape(turns * 8, tok)

    def build_left(row, side):
        left[side] = left_rows(pairs_of(row, side), turns)

    def build_base(row, side, c, pair):
        line = jnp.broadcast_to(filt[pl.ds(row + side * GROUP + c, 1), :], (8, length))
        steps = []
        for a in (2 * pair, 2 * pair + 1):
            shifted = pltpu.roll(line, 8 * a, 1, stride=1, stride_axis=0)
            late = lax.broadcasted_iota(
                jnp.int32, (8, LANES), 1
            ) >= 8 * a + lax.broadcasted_iota(jnp.int32, (8, LANES), 0)
            steps.append(
                jnp.concatenate(
                    [jnp.where(late, shifted[:, :LANES], 0.0), shifted[:, LANES:]], axis=1
                )
            )
        at = c * FINE + 16 * pair
        base[side, at : at + 16, LANES:] = jnp.concatenate(steps, axis=0).astype(BF16)

    jobs = [(c, pair) for c in range(GROUP) for pair in range(FINE // 16)]

    def multiply(side, k):
        start = k * tok
        right = jnp.concatenate(
            [
                base[side, :, LANES + start : LANES + start + tok],
                base[side, :, start : start + tok],
            ],
            axis=0,
        )
        count = turns - k // 2
        out = jnp.dot(left[side, : 32 * count], right, preferred_element_type=F32)
        for m in range(count):
            at = slice(start + 2 * tok * m, start + 2 * tok * m + tok)
            piece = out[32 * m : 32 * m + 32]
            if k < 2:
                total[side, :, at] = piece
            else:
                total[side, :, at] += piece

    def summed(side):
        run = total[side, 24:32]
        for e in (2, 1, 0):
            run = total[side, 8 * e : 8 * e + 8] + delayed(run, FINE)
        return run

    build_left(0, 0)
    for job in jobs:
        build_base(0, 0, *job)

    def unit(index, carry):
        done = []
        for part in range(2):
            row = index * 16 + 8 * part
            sums = []
            for side in range(2):
                if side == 0:
                    after = row
                elif part == 0:
                    after = row + 8
                else:
                    after = jnp.minimum(row + 8, lanes - 8)
                build_left(after, 1 - side)
                for k in range(blocks):
                    for at, job in enumerate(jobs):
                        if at * blocks // len(jobs) == k:
                            build_base(after, 1 - side, *job)
                    multiply(side, k)
                sums.append(summed(side))
            upper = lax.broadcasted_iota(jnp.int32, (8, length), 0) < 4
            even, odd = halves(sums[0], sums[1], upper)
            conv = even + jnp.concatenate(
                [jnp.zeros((8, tok), F32), odd[:, : length - tok]], axis=1
            )
            here = pl.ds(pl.multiple_of(row, 8), 8)
            skip = jnp.concatenate([skip_ref[here, :]] * (tok // LANES), axis=1)
            done.append(
                [conv[:, h * tok : (h + 1) * tok] + skip * prod[h, here, :] for h in range(blocks)]
            )
        for h in range(blocks):
            held[h, pl.ds(pl.multiple_of(index * 16, 16), 16), :] = jnp.concatenate(
                [done[0][h], done[1][h]], axis=0
            ).astype(BF16)
        return carry

    lax.fori_loop(0, units, unit, 0)
    for j, out_ref in enumerate(out_refs):
        for i in range(out_ref.shape[0]):
            out_ref[i] = held[at_ref[0] ^ (out_ref.shape[0] * j + i)]


def long_conv(arrays, skip_rows, later, blocks, near, position, cost=BRIEF):
    _, _, lanes, tok = arrays[0].shape
    length = blocks * tok
    whole = lambda array: pl.BlockSpec(array.shape, lambda i, at: (0,) * len(array.shape))
    out_shape = [jax.ShapeDtypeStruct((near, lanes, tok), BF16)] * (blocks // near) + [DONE]
    return pl.pallas_call(
        conv_kernel,
        grid_spec=pltpu.PrefetchScalarGridSpec(
            num_scalar_prefetch=1,
            grid=(1,),
            in_specs=[whole(skip_rows), corner(later)] + [whole(array) for array in arrays],
            out_specs=[whole(array) for array in out_shape],
            scratch_shapes=[
                pltpu.VMEM((lanes, length), F32),
                pltpu.VMEM((blocks, lanes, tok), F32),
                pltpu.VMEM((2, GROUP * FINE, LANES + length), BF16),
                pltpu.VMEM((2, 16 * blocks, 2 * LANES), BF16),
                pltpu.VMEM((2, 32, length), F32),
                pltpu.VMEM((blocks, lanes, tok), BF16),
            ],
        ),
        out_shape=out_shape,
        compiler_params=pltpu.CompilerParams(vmem_limit_bytes=VMEM_BYTES),
        cost_estimate=cost,
        name="long_conv",
    )(position, skip_rows, later, *arrays)


def gated_kernel(at_ref, gate_ref, halo_ref, taps_ref, *refs):
    held = refs[-1]
    blocks, narrow, tok = held.shape
    near = blocks // refs[0].shape[0]
    mixed_refs, refs = refs[:near], refs[near:-1]
    gated_ref, squares_ref = refs[-2:]
    count = WIDE // narrow
    step = pl.program_id(0)

    @pl.when(step == 0)
    def _():
        for i, mixed_ref in enumerate(mixed_refs):
            for j in range(mixed_ref.shape[0]):
                held[at_ref[0] ^ (near * j + i)] = mixed_ref[j]

    halo = halo_ref[...].astype(F32)
    gate = short_conv(gate_ref[...].astype(F32), halo[2 * HALO :], taps_ref[...])
    mixed = held[pl.ds(step * count, count)].reshape(WIDE, tok)
    gated = gate * mixed.astype(F32).T
    gated_ref[...] = gated
    squares = gated * gated
    part = squares[:, :LANES]
    for at in range(LANES, WIDE, LANES):
        part = part + squares[:, at : at + LANES]
    turned = jnp.sum(part.T.reshape(LANES // 8, 8, part.shape[0]), axis=0)

    @pl.when(step == 0)
    def _():
        squares_ref[...] = refs[0][...] + turned if len(refs) > 2 else turned

    @pl.when(step > 0)
    def _():
        squares_ref[...] += turned


def gated_of(gate_in, halo, gate_short, mixed, start, before, position):
    tok, full = gate_in.shape
    far, narrow, _ = mixed[0].shape
    near = len(mixed)
    width = near * far * narrow
    first = start // WIDE
    column = lambda rows: pl.BlockSpec((rows, WIDE), lambda i, at: (0, first + i))
    sums = pl.BlockSpec((8, tok), lambda i, at: (0, 0))
    more = [] if before is None else [sums, pl.BlockSpec(memory_space=pl.ANY)]
    return pl.pallas_call(
        gated_kernel,
        grid_spec=pltpu.PrefetchScalarGridSpec(
            num_scalar_prefetch=1,
            grid=(width // WIDE,),
            in_specs=[column(tok), column(3 * HALO), column(3)]
            + [pl.BlockSpec(mixed[0].shape, lambda i, at: (0, 0, 0))] * near
            + more,
            out_specs=[column(tok), sums],
            scratch_shapes=[pltpu.VMEM((near * far, narrow, tok), BF16)],
        ),
        out_shape=[
            jax.ShapeDtypeStruct((tok, full), F32),
            jax.ShapeDtypeStruct((8, tok), F32),
        ],
        input_output_aliases={5 + near: 0} if more else {},
        compiler_params=pltpu.CompilerParams(vmem_limit_bytes=VMEM_BYTES),
        cost_estimate=BRIEF,
        name="gated_squares",
    )(
        position,
        gate_in,
        halo,
        gate_short,
        *mixed,
        *(() if before is None else (before[1], before[0])),
    )


def norm_kernel(channels, gated_ref, gain_ref, *refs):
    sums, out_ref = refs[:-1], refs[-1]
    total = sums[0][...]
    for other in sums[1:]:
        total = total + other[...]
    total = jnp.sum(total, axis=0, keepdims=True)
    scale = lax.rsqrt(total / channels + 1e-06)
    scale = jnp.broadcast_to(scale, (LANES, scale.shape[1])).T
    scale = jnp.concatenate([scale] * (WIDE // LANES), axis=1)
    out_ref[...] = (gated_ref[...] * gain_ref[...] * scale).astype(BF16)


def normed(gated, squares, norm_gain, channels):
    tok, width = gated.shape
    column = lambda rows: pl.BlockSpec((rows, WIDE), lambda i: (0, i))
    return pl.pallas_call(
        functools.partial(norm_kernel, channels),
        grid=(width // WIDE,),
        in_specs=[column(tok), column(1)]
        + [pl.BlockSpec((8, tok), lambda i: (0, 0))] * len(squares),
        out_specs=column(tok),
        out_shape=jax.ShapeDtypeStruct((tok, width), BF16),
        compiler_params=pltpu.CompilerParams(vmem_limit_bytes=VMEM_BYTES),
        cost_estimate=BRIEF,
        name="normed",
    )(gated, norm_gain, *squares)


def local(
    gate_in, key_in, value_in, long_filter, gate_short, key_short, value_short, skip_gain, norm_gain
):
    tok, width = value_in.shape
    blocks = lax.axis_size("seq")
    groups = lax.axis_size("ch")
    place = lax.axis_index("seq")
    position = jnp.full((1,), place, jnp.int32)
    narrow = width // blocks // PARTS
    starts = [at * narrow * blocks for at in range(PARTS)]
    exchange = lambda rows: lax.all_to_all(rows, "seq", split_axis=0, concat_axis=0, tiled=True)
    natural = jnp.zeros((1,), jnp.int32)
    pack = lambda wants, start, near, origin, later: packed(
        wants,
        ([long_filter] if "filter" in wants else [])
        + ([key_in, value_in, halo, key_short, value_short] if "product" in wants else []),
        later,
        (start, narrow, blocks),
        near,
        origin,
    )

    def skip_of(start):
        skip = lax.dynamic_slice_in_dim(skip_gain, start + place * narrow, narrow, 0)
        return jnp.broadcast_to(skip[:, None], (narrow, LANES))

    halo = passed_along(tails((key_in, value_in, gate_in)), "seq", 1)
    *lines, ended = pack(("filter",), starts[0], NEAR, position, [])
    lines = swap_far(lines)
    *product, _ = pack(("product",), starts[0], NEAR, position, [ended])
    came = swap_far(product)
    filters = swap_near(lines, came[2])
    products = swap_near(came, lines[2])
    later = [filters[2], products[2]]
    second, done = pack(("filter", "product"), starts[1], blocks, natural, later)
    second = exchange(second)
    *lines, ended = long_conv(filters + products, skip_of(starts[0]), done, blocks, NEAR, position)
    lines = swap_far(lines)
    cost = pl.CostEstimate(
        flops=2 * width * tok * tok * blocks, bytes_accessed=6 * tok * width, transcendentals=0
    )
    last, done = long_conv([second], skip_of(starts[1]), ended, blocks, blocks, natural, cost)
    lines, last, done = lax.optimization_barrier((lines, last, done))
    first = swap_near(lines, done)
    last = exchange(last)
    gated = gated_of(gate_in, halo, gate_short, first, starts[0], None, position)
    gated = gated_of(gate_in, halo, gate_short, [last], starts[1], gated, natural)
    gated, squares = gated
    sums = [squares]
    for by in range(1, groups):
        sums.append(lax.ppermute(squares, "ch", [(i, (i + by) % groups) for i in range(groups)]))
    return normed(gated, sums, norm_gain[None, :], width * groups)


def solution(mesh):
    return jax.shard_map(
        local,
        mesh=mesh,
        in_specs=(
            P("seq", "ch"),
            P("seq", "ch"),
            P("seq", "ch"),
            P("seq", "ch"),
            P(None, "ch"),
            P(None, "ch"),
            P(None, "ch"),
            P("ch"),
            P("ch"),
        ),
        out_specs=P("seq", "ch"),
        check_vma=False,
    )
```
